32 devices in a mesh: path: 8 (over z, y), shard: 4 (over x, core).
Axes of the slice: x: 2, y: 2, z: 4, core: 2. Of those that a mesh axis runs over, the one named last changes fastest.
Arguments:
- tokens: bfloat16 [1536, 2112], P('path'), may hold values from -6 to 6
- out_grad: bfloat16 [1536, 2112], P('path'), may hold values from -0.059814453 to 0.059814453
- doc_lengths: int32 [8, 24], P('path'), may hold values from 1 to 16, 192 in all within a row
- doc_paths: int32 [8, 24], P('path'), may hold values from 0 to 7
- membership: int32 [8, 2], replicated, may hold values from 0 to 3
- up_master: float32 [4, 2112, 8192], P(None, 'path', 'shard'), may hold values from -0.9574271 to 0.9574271
- down_master: float32 [4, 2112, 8192], P(None, 'path', 'shard'), may hold values from -0.4861359 to 0.4861359
- up_moment: bfloat16 [4, 2112, 8192], P(None, 'path', 'shard'), may hold values from -0.059814453 to 0.059814453
- down_moment: bfloat16 [4, 2112, 8192], P(None, 'path', 'shard'), may hold values from -0.059814453 to 0.059814453
Outputs:
- new_up_master: float32 [4, 2112, 8192], P(None, 'path', 'shard')
- new_down_master: float32 [4, 2112, 8192], P(None, 'path', 'shard')
- new_up_moment: bfloat16 [4, 2112, 8192], P(None, 'path', 'shard')
- new_down_moment: bfloat16 [4, 2112, 8192], P(None, 'path', 'shard')
The draws below stay inside these ranges and needn't reach their ends.
All inputs are finite; a program needn't handle non-finite values.
Results may differ from the reference program's by a relative error of at most 0.005.
The reference program's roundings to bfloat16 on the way (of `rows_in`, `grads_in`, `normed`, `hidden_b` and `dpre`) count: a program that leaves them out, or rounds other values in their place, can miss the bound.
Values may be sent and summed in bfloat16 or wider, within the bound.
No kernel may reach another device: no remote copies, remote signals or barrier semaphores. Data moves between devices by JAX's collectives and lax.ppermute only.
A program may use at most 128 MiB of HBM per device.

```python
import math
import jax
import jax.numpy as jnp
import numpy as np
from jax import lax

D = 2112
FF = 8192
MODS = 4
DOCS = 24
TOK_DEV = 192
MOST = 16
PATHS = 8
CAP = 24
SLOTS = 192
ROWS = 1536


def ramped(key, fan_value, spread, wobble):
    first, second = jax.random.split(key)
    base = jax.random.truncated_normal(first, -4.0, 4.0, (MODS, D, FF), jnp.float32) / math.sqrt(fan_value)
    place = jnp.arange(FF, dtype=jnp.float32) / FF
    factor = jnp.exp(math.log(spread) * place) * jax.random.uniform(second, (FF,), jnp.float32, 1.0 / wobble, wobble)
    return base * factor * 0.8


def draw_up_master(key, part):
    key = jax.random.fold_in(key, 5)
    return ramped(key, D, 3.0, 1.3)


def draw_down_master(key, part):
    key = jax.random.fold_in(key, 9)
    return ramped(key, FF, 3.0, 1.3)


def place_ends(drawn, key, smallest, largest):
    spot = [jax.random.randint(jax.random.fold_in(key, axis), (), 0, length) for axis, length in enumerate(drawn.shape)]
    widest = drawn.shape.index(max(drawn.shape))
    neighbour = spot[:widest] + [(spot[widest] + 1) % drawn.shape[widest]] + spot[widest + 1:]
    return drawn.at[tuple(spot)].set(smallest).at[tuple(neighbour)].set(largest)


def steps_of(key, dims, cuts, least, top_value):
    loudness = 1.0
    for axis_at, blocks in cuts:
        draws = jax.random.uniform(jax.random.fold_in(jax.random.fold_in(key, 6), axis_at), (blocks,), jnp.float32, least / len(cuts), top_value / len(cuts))
        loudness = loudness * jnp.repeat(jnp.exp(draws), dims[axis_at] // blocks).reshape((-1,) + (1,) * (len(dims) - 1 - axis_at))
    return loudness


def cumulative_ranks(amount, skew):
    loads = [(1 << 20) // math.isqrt(grade ** skew) + 1 for grade in range(1, amount + 1)]
    scale = 1 + sum(loads) // (1 << 30)
    return np.cumsum(np.array([max(1, weight // scale) for weight in loads]))


def skewed_ids(own_key, dims, count, lean):
    grid = cumulative_ranks(count, lean)
    lot = jax.random.randint(jax.random.fold_in(own_key, 1), dims, 0, int(grid[count - 1]))
    rank = jnp.searchsorted(jnp.asarray(grid, jnp.int32), lot, side="right")
    return jax.random.permutation(jax.random.fold_in(own_key, 2), count)[rank].astype(jnp.int32)


def split_up(amount, total, most, lean):
    loads = [(1 << 20) // math.isqrt(standing ** lean) + 1 for standing in range(2, amount + 1)]
    rest, given = total - most - (amount - 1), [1] * (amount - 1)
    while rest > 0:
        candidates = [i for i in range(amount - 1) if given[i] < most]
        pool, remaining = sum([loads[i] for i in candidates]), rest
        for i in candidates:
            addition = min(most - given[i], max(1, remaining * loads[i] // pool), rest)
            given[i] = given[i] + addition
            rest = rest - addition
    return np.array([most] + given)


def ragged_sizes(key, number_of, total, bound, skew):
    if number_of == 2:
        one = jax.random.randint(key, (), max(1, total - bound), min(bound, total - 1) + 1)
        return jnp.stack([one, total - one])
    sizes = jnp.asarray(split_up(number_of, total, bound, skew), jnp.int32)
    twos = (number_of - 1) // 2
    giver, receiver = sizes[1:1 + 2 * twos:2], sizes[2:2 + 2 * twos:2]
    margin = jnp.minimum(giver - 1, bound - receiver)
    moved = jax.random.randint(jax.random.fold_in(key, 1), (twos,), 0, 1 << 20) % (margin + 1)
    sizes = sizes.at[1:1 + 2 * twos:2].set(giver - moved).at[2:2 + 2 * twos:2].set(receiver + moved)
    return sizes[jax.random.permutation(jax.random.fold_in(key, 2), number_of)]


def noise(rng, extent, width, bound, pieces=(), held_as=jnp.bfloat16):
    result = jax.random.normal(rng, extent, jnp.float32) * width
    if len(pieces) > 0:
        result = steps_of(rng, extent, pieces, -0.22, 0.18) * result
    return jnp.clip(result, min=-bound, max=bound).astype(held_as)


def setup_inputs(seed: int = 0) -> dict:
    streams_of = jax.random.split(jax.random.key(seed), 10)
    tokens = noise(streams_of[0], (ROWS, D), 1.0, 6.0, ((0, 8),))
    out_grad = noise(streams_of[1], (ROWS, D), 0.01, 0.059814453, ((0, 8),))
    doc_lengths = jax.vmap(lambda own: ragged_sizes(own, DOCS, TOK_DEV, MOST, 2))(jax.random.split(streams_of[2], PATHS)).reshape((PATHS, DOCS)).astype(jnp.int32)
    doc_paths = place_ends(skewed_ids(streams_of[3], (PATHS, DOCS), PATHS, 1), jax.random.fold_in(streams_of[3], 3), 0, PATHS - 1).astype(jnp.int32)
    membership = place_ends(jax.random.randint(streams_of[4], (PATHS, 2), 0, MODS), jax.random.fold_in(streams_of[4], 1), 0, MODS - 1).astype(jnp.int32)
    up_master = draw_up_master(jax.random.fold_in(streams_of[9], 71), 0)
    down_master = draw_down_master(jax.random.fold_in(streams_of[9], 71), 0)
    up_moment = noise(streams_of[7], (MODS, D, FF), 0.01, 0.059814453, ((1, 8), (2, 4)))
    down_moment = noise(streams_of[8], (MODS, D, FF), 0.01, 0.059814453, ((1, 8), (2, 4)))
    return {"tokens": tokens, "out_grad": out_grad, "doc_lengths": doc_lengths, "doc_paths": doc_paths, "membership": membership, "up_master": up_master, "down_master": down_master, "up_moment": up_moment, "down_moment": down_moment}


norm_epsilon = 1e-06
hidden_epsilon = 1e-05
adam_epsilon = 0.001
inner_rate = 0.05
decay_rate = 0.1
outer_rate = 0.7
momentum_coef = 0.9
gelu_coef = 0.7978845608
cubic_coef = 0.044715

def gelu_pair(values):
    inner = gelu_coef * (values + cubic_coef * values * values * values)
    tangent = jnp.tanh(inner)
    activated = 0.5 * values * (1.0 + tangent)
    slopes = 0.5 * (1.0 + tangent) + 0.5 * values * (1.0 - tangent * tangent) * gelu_coef * (1.0 + 3.0 * cubic_coef * values * values)
    return (activated, slopes)

def placing_matrix(lengths, targets, row_count, path_count, capacity):
    ends = jnp.cumsum(lengths)
    row_ids = jnp.arange(row_count, dtype=jnp.int32)
    doc_of_row = lax.optimization_barrier(jnp.sum((row_ids[:, None] >= ends[None, :]).astype(jnp.int32), axis=1))
    doc_hit = doc_of_row[:, None] == jnp.arange(lengths.shape[0], dtype=jnp.int32)[None, :]
    row_path = lax.optimization_barrier(jnp.sum(jnp.where(doc_hit, targets[None, :], 0), axis=1)).astype(jnp.int32)
    path_hit = (row_path[:, None] == jnp.arange(path_count, dtype=jnp.int32)[None, :]).astype(jnp.int32)
    ranks = lax.optimization_barrier(jnp.sum((jnp.cumsum(path_hit, axis=0) - 1) * path_hit, axis=1)).astype(jnp.int32)
    slots = jnp.where(ranks < capacity, row_path * capacity + ranks, -1)
    return (jnp.arange(path_count * capacity, dtype=jnp.int32)[:, None] == slots[None, :]).astype(jnp.bfloat16)

def adam_delta(gradient, weight):
    update = gradient / (jnp.abs(gradient) + adam_epsilon) + decay_rate * weight.astype(jnp.float32)
    return (-inner_rate * update).astype(jnp.bfloat16)

def outer_update(master, moment, summed, counts):
    pseudo = -summed / jnp.maximum(counts, 1.0)[:, None, None]
    buffer = momentum_coef * moment.astype(jnp.float32) + pseudo
    return (master - outer_rate * (pseudo + momentum_coef * buffer), buffer.astype(jnp.bfloat16))

def path_step(rows_in, grads_in, up_weight, down_weight):
    rows_float = rows_in.astype(jnp.float32)
    normed = (rows_float * lax.rsqrt(lax.optimization_barrier(jnp.mean(rows_float * rows_float, axis=1, keepdims=True)) + norm_epsilon)).astype(jnp.bfloat16)
    pre = jnp.dot(normed, up_weight, preferred_element_type=jnp.float32)
    activated, slopes = gelu_pair(pre)
    scale = jnp.sqrt(lax.optimization_barrier(jnp.mean(activated * activated, axis=1, keepdims=True)) + hidden_epsilon)
    hidden = activated / scale
    hidden_b = hidden.astype(jnp.bfloat16)
    grad_down = jnp.dot(grads_in.T, hidden_b, preferred_element_type=jnp.float32)
    back = jnp.dot(grads_in, down_weight, preferred_element_type=jnp.float32)
    mixing = lax.optimization_barrier(jnp.mean(back * hidden, axis=1, keepdims=True))
    dpre = ((back - hidden * mixing) / scale * slopes).astype(jnp.bfloat16)
    grad_up = jnp.dot(normed.T, dpre, preferred_element_type=jnp.float32)
    return (adam_delta(grad_up, up_weight), adam_delta(grad_down, down_weight))

def reference(tokens, out_grad, doc_lengths, doc_paths, membership, up_master, down_master, up_moment, down_moment):
    placing = jax.vmap(lambda lengths, targets: placing_matrix(lengths, targets, TOK_DEV, PATHS, CAP))(doc_lengths, doc_paths)
    placing_float = placing.astype(jnp.float32)
    token_groups = tokens.reshape(PATHS, TOK_DEV, D).astype(jnp.float32)
    grad_groups = out_grad.reshape(PATHS, TOK_DEV, D).astype(jnp.float32)
    sent_rows = jnp.einsum('gst,gtd->gsd', placing_float, token_groups).astype(jnp.bfloat16)
    sent_grads = jnp.einsum('gst,gtd->gsd', placing_float, grad_groups).astype(jnp.bfloat16)

    def visit(carry, path_id):
        sums_up, sums_down = carry
        start = (path_id * CAP).astype(jnp.int32)
        rows_in = lax.dynamic_slice_in_dim(sent_rows, start, CAP, 1).reshape(SLOTS, D)
        grads_in = lax.dynamic_slice_in_dim(sent_grads, start, CAP, 1).reshape(SLOTS, D)
        up_id = membership[path_id, 0]
        down_id = membership[path_id, 1]
        up_weight = up_master[up_id].astype(jnp.bfloat16)
        down_weight = down_master[down_id].astype(jnp.bfloat16)
        delta_up, delta_down = path_step(rows_in, grads_in, up_weight, down_weight)
        sums_up = sums_up.at[up_id].add(delta_up.astype(jnp.float32))
        sums_down = sums_down.at[down_id].add(delta_down.astype(jnp.float32))
        return ((sums_up, sums_down), None)
    zeros_sum = jnp.zeros((MODS, D, FF), jnp.float32)
    (sums_up, sums_down), unused = lax.scan(visit, (zeros_sum, zeros_sum), jnp.arange(PATHS, dtype=jnp.int32))
    module_ids = jnp.arange(MODS, dtype=jnp.int32)
    counts_up = lax.optimization_barrier(jnp.sum((membership[:, 0][None, :] == module_ids[:, None]).astype(jnp.float32), axis=1))
    counts_down = lax.optimization_barrier(jnp.sum((membership[:, 1][None, :] == module_ids[:, None]).astype(jnp.float32), axis=1))
    new_up_master, new_up_moment = outer_update(up_master, up_moment, sums_up, counts_up)
    new_down_master, new_down_moment = outer_update(down_master, down_moment, sums_down, counts_down)
    return (new_up_master, new_down_master, new_up_moment, new_down_moment)
```

```python
import functools

import jax
import jax.numpy as jnp
from jax import lax
from jax.experimental import pallas as pl
from jax.experimental.pallas import tpu as pltpu
from jax.sharding import PartitionSpec as P

norm_epsilon = 1e-06
hidden_epsilon = 1e-05
adam_epsilon = 0.001
inner_rate = 0.05
decay_rate = 0.1
outer_rate = 0.7
momentum_coef = 0.9
vmem_limit = 56 * 1024 * 1024
small_cost = pl.CostEstimate(flops=1, bytes_accessed=1, transcendentals=0)
gelu_coef = 0.7978845608
cubic_coef = 0.044715


def gelu_pair(values):
    inner = gelu_coef * (values + cubic_coef * values * values * values)
    tangent = jnp.tanh(inner)
    activated = 0.5 * values * (1.0 + tangent)
    slopes = 0.5 * (1.0 + tangent) + 0.5 * values * (1.0 - tangent * tangent) * gelu_coef * (
        1.0 + 3.0 * cubic_coef * values * values
    )
    return (activated, slopes)


def placing_matrix(lengths, targets, row_count, path_count, capacity, first_slot, slot_count):
    ends = jnp.cumsum(lengths)
    row_ids = jnp.arange(row_count, dtype=jnp.int32)
    doc_of_row = jnp.sum((row_ids[:, None] >= ends[None, :]).astype(jnp.int32), axis=1)
    doc_hit = doc_of_row[:, None] == jnp.arange(lengths.shape[0], dtype=jnp.int32)[None, :]
    row_path = jnp.sum(jnp.where(doc_hit, targets[None, :], 0), axis=1)
    path_hit = (row_path[:, None] == jnp.arange(path_count, dtype=jnp.int32)[None, :]).astype(
        jnp.int32
    )
    ranks = jnp.sum((jnp.cumsum(path_hit, axis=0) - 1) * path_hit, axis=1)
    slots = jnp.where(ranks < capacity, row_path * capacity + ranks, -1)
    wanted = first_slot + jnp.arange(slot_count, dtype=jnp.int32)
    return (wanted[:, None] == slots[None, :]).astype(jnp.bfloat16)


def outgoing_kernel(table_ref, *refs):
    half = len(refs) // 2
    for master_ref, out_ref in zip(refs[:half], refs[half:]):
        out_ref[...] = master_ref[...].astype(jnp.bfloat16)


def outgoing_weights(member, team, master):
    count, owned, width = master.shape
    block = width // team
    masks = range(1, team)
    return pl.pallas_call(
        outgoing_kernel,
        out_shape=[jax.ShapeDtypeStruct((count, owned, block), jnp.bfloat16) for _ in masks],
        grid_spec=pltpu.PrefetchScalarGridSpec(
            num_scalar_prefetch=1,
            grid=(count,),
            in_specs=[
                pl.BlockSpec((1, owned, block), lambda i, t, mask=mask: (i, 0, t[0] ^ mask))
                for mask in masks
            ],
            out_specs=[pl.BlockSpec((1, owned, block), lambda i, t: (i, 0, 0)) for _ in masks],
        ),
        compiler_params=pltpu.CompilerParams(vmem_limit_bytes=vmem_limit),
        cost_estimate=small_cost,
        name="outgoing_weights",
    )(member.reshape(1), *[master for _ in masks])


def arranged_kernel(team, table_ref, *refs):
    pieces, (out_ref, by_source_ref, rows_ref) = refs[: 2 * team], refs[2 * team :]
    member, group, quarter = table_ref[0], table_ref[1], table_ref[2]
    _, groups, _, _, capacity, _ = pieces[0].shape
    sources = groups * team
    owned = out_ref.shape[3]

    def collect(half):
        for mask in range(team):
            for offset in range(groups):
                source = lax.rem(group + groups - offset, groups) * team + (member ^ mask)
                by_source_ref[source] = half[mask][0, offset, 0, 0].astype(jnp.float32)

    mine = ((pl.program_id(0) // (pl.num_programs(0) // 4)) ^ quarter) % 2 == 0

    @pl.when(mine)
    def _():
        collect(pieces[:team])

    @pl.when(jnp.logical_not(mine))
    def _():
        collect(pieces[team:])

    for source in range(sources):
        rows_ref[source * capacity : (source + 1) * capacity, :] = by_source_ref[source]
    for block in range(team):
        out_ref[0, block] = rows_ref[:, block * owned : (block + 1) * owned].astype(jnp.bfloat16)


def arranged(which, table, team, paths, mine, theirs):
    _, groups, _, kept, capacity, depth = mine[0].shape
    slots = paths * capacity
    owned = depth // team
    piece = pl.BlockSpec(
        (1, groups, 1, 1, capacity, depth),
        lambda p, t: ((lax.div(p, kept) ^ t[2]) // 2, 0, which, lax.rem(p, kept), 0, 0),
    )
    return pl.pallas_call(
        functools.partial(arranged_kernel, team),
        out_shape=jax.ShapeDtypeStruct((paths, team, slots, owned), jnp.bfloat16),
        grid_spec=pltpu.PrefetchScalarGridSpec(
            num_scalar_prefetch=1,
            grid=(paths,),
            in_specs=[piece] * (2 * team),
            out_specs=pl.BlockSpec((1, team, slots, owned), lambda p, t: (p, 0, 0, 0)),
            scratch_shapes=[
                pltpu.VMEM((groups * team, capacity, depth), jnp.float32),
                pltpu.VMEM((slots, depth), jnp.float32),
            ],
        ),
        compiler_params=pltpu.CompilerParams(vmem_limit_bytes=vmem_limit),
        cost_estimate=small_cost,
        name="arranged",
    )(table, *mine, *theirs)


def product_kernel(team, listed, table_ref, rows_ref, own_ref, *refs):
    received, out_ref = refs[:-1], refs[-1]
    member = table_ref[0]
    module = table_ref[1 + listed + pl.program_id(0)]
    total = jnp.dot(
        rows_ref[0, member],
        own_ref[module].astype(jnp.bfloat16),
        preferred_element_type=jnp.float32,
    )
    for mask in range(1, team):
        total += jnp.dot(
            rows_ref[0, member ^ mask],
            received[mask - 1][module],
            preferred_element_type=jnp.float32,
        )
    out_ref[0] = total


def products(member, paths, modules, rows, master, received):
    _, team, slots, owned = rows.shape
    count, _, block = received[0].shape
    listed = paths.shape[0]
    table = jnp.concatenate([member.reshape(1), paths, jnp.take(modules, paths)])
    weights = pl.BlockSpec((count, owned, block), lambda i, t: (0, 0, 0))
    return pl.pallas_call(
        functools.partial(product_kernel, team, listed),
        out_shape=jax.ShapeDtypeStruct((listed, slots, block), jnp.float32),
        grid_spec=pltpu.PrefetchScalarGridSpec(
            num_scalar_prefetch=1,
            grid=(listed,),
            in_specs=[
                pl.BlockSpec((1, team, slots, owned), lambda i, t: (t[1 + i], 0, 0, 0)),
                pl.BlockSpec((count, owned, block), lambda i, t: (0, 0, t[0])),
            ]
            + [weights] * (team - 1),
            out_specs=pl.BlockSpec((1, slots, block), lambda i, t: (i, 0, 0)),
        ),
        compiler_params=pltpu.CompilerParams(vmem_limit_bytes=vmem_limit),
        cost_estimate=small_cost,
        name="products",
    )(table, rows, master, *received)


def update_kernel(blocks, groups, tiles, previous_count, table_ref, left_ref, *refs):
    rights = refs[: blocks * groups]
    master_ref, moment_ref = refs[blocks * groups : blocks * groups + 2]
    new_master_ref, new_moment_ref, sums_ref, decay_ref = refs[blocks * groups + 2 + previous_count :]
    paths = left_ref.shape[0]
    sums_ref[...] = jnp.zeros_like(sums_ref)
    decay_ref[...] = decay_rate * master_ref[...].astype(jnp.bfloat16).astype(jnp.float32)

    def accumulate(block):
        for group in range(groups):
            right_ref = rights[block * groups + group]
            for member in range(right_ref.shape[0]):
                path = table_ref[blocks + group] + member
                module = table_ref[blocks + groups + path]
                gradient = jnp.dot(
                    left_ref[path], right_ref[member], preferred_element_type=jnp.float32
                )
                step = gradient * pl.reciprocal(jnp.abs(gradient) + adam_epsilon)
                update = step + decay_ref[module]
                sums_ref[module] += (-inner_rate * update).astype(jnp.bfloat16).astype(jnp.float32)

    for block in range(blocks):
        pl.when(pl.program_id(0) // tiles == block)(functools.partial(accumulate, block))

    for module in range(master_ref.shape[0]):
        count = lax.fori_loop(
            0,
            paths,
            lambda path, total: total
            + (table_ref[blocks + groups + path] == module).astype(jnp.int32),
            0,
        )
        divisor = jnp.maximum(count, 1).astype(jnp.float32)
        pseudo = -sums_ref[module] / divisor
        buffer = momentum_coef * moment_ref[module].astype(jnp.float32) + pseudo
        new_master_ref[module] = master_ref[module] - outer_rate * (pseudo + momentum_coef * buffer)
        new_moment_ref[module] = buffer.astype(jnp.bfloat16)


def updated(columns, firsts, modules, left, rights, master, moment, previous):
    paths, owned, slots = left.shape
    count, _, width = master.shape
    blocks, groups = len(rights), len(rights[0])
    members, _, block = rights[0][0].shape
    tile = min(256, block)
    tiles = block // tile
    table = jnp.concatenate([jnp.stack(columns), firsts, modules])
    module_spec = pl.BlockSpec(
        (count, owned, tile),
        lambda f, t: (0, 0, t[lax.div(f, tiles)] * tiles + lax.rem(f, tiles)),
    )
    right_specs = [
        pl.BlockSpec(
            (members, slots, tile),
            lambda f, t, start=index * tiles: (0, 0, jnp.clip(f - start, 0, tiles - 1)),
        )
        for index in range(blocks)
        for _ in range(groups)
    ]
    first_previous = 4 + blocks * groups
    return pl.pallas_call(
        functools.partial(update_kernel, blocks, groups, tiles, len(previous)),
        out_shape=(
            jax.ShapeDtypeStruct(master.shape, jnp.float32),
            jax.ShapeDtypeStruct(master.shape, jnp.bfloat16),
        ),
        grid_spec=pltpu.PrefetchScalarGridSpec(
            num_scalar_prefetch=1,
            grid=(blocks * tiles,),
            in_specs=[pl.BlockSpec((paths, owned, slots), lambda f, t: (0, 0, 0))]
            + right_specs
            + [module_spec, module_spec]
            + [pl.BlockSpec(memory_space=pl.ANY)] * len(previous),
            out_specs=[module_spec, module_spec],
            scratch_shapes=[pltpu.VMEM((count, owned, tile), jnp.float32)] * 2,
        ),
        input_output_aliases={first_previous + i: i for i in range(len(previous))},
        compiler_params=pltpu.CompilerParams(vmem_limit_bytes=vmem_limit),
        cost_estimate=small_cost,
        name="updated",
    )(table, left, *[right for listed in rights for right in listed], master, moment, *previous)


def on_device(
    tokens,
    out_grad,
    doc_lengths,
    doc_paths,
    membership,
    up_master,
    down_master,
    up_moment,
    down_moment,
):
    path_count = lax.axis_size("path")
    shard_count = lax.axis_size("shard")
    row_count, features = tokens.shape
    width = up_master.shape[2]
    hidden_units = width * shard_count
    capacity = row_count // path_count
    slots = path_count * capacity
    kept = path_count // 4
    up_modules, down_modules = membership[:, 0], membership[:, 1]

    team = 4
    groups = path_count // team
    me = lax.axis_index("path")
    member, group = me % team, me // team
    quarter = lax.axis_index("shard") % 4
    bits = (2, 1)

    def trade(value, mask):
        return lax.ppermute(value, "path", [(i, i ^ mask) for i in range(path_count)])

    def move(value, offset):
        if offset == 0:
            return value
        return lax.ppermute(
            value, "path", [(i, (i + team * offset) % path_count) for i in range(path_count)]
        )

    def share(value, mask):
        return lax.ppermute(value, "shard", [(i, i ^ mask) for i in range(shard_count)])

    def tie(*values):
        return lax.optimization_barrier(values)

    up_out = outgoing_weights(member, team, up_master)
    up_beside, up_near = trade(up_out[0], 1), trade(up_out[1], 2)

    placing = placing_matrix(
        doc_lengths[0],
        doc_paths[0],
        row_count,
        path_count,
        capacity,
        quarter * kept * capacity,
        kept * capacity,
    )
    rows = jnp.dot(placing, tokens, preferred_element_type=jnp.float32)
    grads = jnp.dot(placing, out_grad, preferred_element_type=jnp.float32).astype(jnp.bfloat16)
    normed = (
        rows * lax.rsqrt(jnp.mean(rows * rows, axis=1, keepdims=True) + norm_epsilon)
    ).astype(jnp.bfloat16)
    depth = features // groups

    sent = jnp.stack([normed, grads]).reshape(2, kept, capacity, features)
    pieces = jnp.stack(
        [
            move(
                lax.dynamic_slice_in_dim(sent, (group + offset) % groups * depth, depth, 3), offset
            )
            for offset in range(groups)
        ]
    )
    near, beside, along = trade(pieces, 2), trade(pieces, 1), share(pieces, 2)
    near, beside, along, up_beside, up_near, across = tie(
        near, beside, along, up_beside, up_near, up_out[2]
    )
    up_across = trade(across, 3)
    near_beside = trade(near, 1)
    near_along, beside_along = share(near, 2), share(beside, 2)
    down_out = outgoing_weights(member, team, down_master)
    near_beside, near_along, beside_along, down_out = tie(
        near_beside, near_along, beside_along, down_out
    )
    down_near = trade(down_out[1], 2)
    mine = [
        jnp.stack(pair)
        for pair in (
            (pieces, along),
            (beside, beside_along),
            (near, near_along),
            (near_beside, share(near_beside, 2)),
        )
    ]
    theirs = [share(value, 1) for value in mine]
    down_beside, down_across = trade(down_out[0], 1), trade(down_out[2], 3)
    place = jnp.stack([member, group, quarter])

    def group_paths(offset):
        return (group + offset) % groups * team + jnp.arange(team, dtype=jnp.int32)

    def part_of(offset, rows, modules, master, weights):
        return products(member, group_paths(offset), modules, rows, master, weights)

    def summed(own, moved):
        for value in moved:
            own = own + value
        return own

    others = range(1, groups)

    def row_sums(values):
        summed = lax.psum(jnp.sum(values, axis=2), "shard")
        for bit in bits:
            summed = summed + trade(summed, bit)
        return summed

    def own_blocks(block):
        return [move(block, offset) for offset in range(groups)]

    firsts = jnp.stack([(group + groups - offset) % groups * team for offset in range(groups)])
    def outer_step(found, results, some_batches, modules, left, master, moment):
        for batch in some_batches:
            results = updated(
                [member ^ mask for mask in batch],
                firsts,
                modules,
                left,
                [found[mask] for mask in batch],
                master,
                moment,
                results,
            )
        return results

    def left_of(rows):
        return lax.dynamic_index_in_dim(rows, member, 1, False).transpose(0, 2, 1)

    def moved(block):
        return [move(block, offset) for offset in others]

    normed_rows = arranged(0, place, team, path_count, mine, theirs)
    normed_rows, down_near = tie(normed_rows, down_near)
    up_operands = (normed_rows, up_modules, up_master, [up_beside, up_near, up_across])
    pre_moved = [move(part_of(offset, *up_operands), offset) for offset in others]
    pre_own = part_of(0, *up_operands)
    late_place, pre_own = tie(place, pre_own)
    grad_rows = arranged(1, late_place, team, path_count, mine, theirs)
    down_operands = (grad_rows, down_modules, down_master, [down_beside, down_near, down_across])
    back_parts = [part_of(offset, *down_operands) for offset in others]
    back_own = part_of(0, *down_operands)
    pre_moved, back_parts = tie(pre_moved, back_parts)
    early = 2
    back_early = [move(part[:early], offset) for part, offset in zip(back_parts, others)]

    activated, slopes = gelu_pair(summed(pre_own, pre_moved))
    scale = jnp.sqrt(row_sums(activated * activated) / hidden_units + hidden_epsilon)[:, :, None]
    hidden = activated / scale
    hidden, back_early = tie(hidden, back_early)
    hidden_b = hidden.astype(jnp.bfloat16)
    near, beside, far = trade(hidden_b, 2), trade(hidden_b, 1), moved(hidden_b)
    far, near, beside, back_parts, back_own = tie(far, near, beside, back_parts, back_own)
    back_late = [move(part[early:], offset) for part, offset in zip(back_parts, others)]
    far_near = [trade(value, 2) for value in far]
    far_beside = [trade(value, 1) for value in far]
    near_beside = trade(near, 1)

    def down_step(results, mask, right):
        return outer_step(
            {mask: right}, results, [[mask]], down_modules, lefts[1], down_master, down_moment
        )

    def up_step(results, mask, right):
        return outer_step(
            {mask: right}, results, [[mask]], up_modules, lefts[0], up_master, up_moment
        )

    lefts = left_of(normed_rows), left_of(grad_rows)
    down_result = down_step((), 0, [hidden_b, *far])
    far_near, far_beside, near_beside, lefts, down_result = tie(
        far_near, far_beside, near_beside, lefts, down_result
    )
    last = [trade(value, 1) for value in far_near]
    back_late, down_result = tie(back_late, down_result)

    back_moved = [jnp.concatenate(pair, axis=0) for pair in zip(back_early, back_late)]
    back = summed(back_own, back_moved)
    mixing = (row_sums(back * hidden) / hidden_units)[:, :, None]
    dpre = ((back - hidden * mixing) / scale * slopes).astype(jnp.bfloat16)
    d_far, d_near, d_beside = moved(dpre), trade(dpre, 2), trade(dpre, 1)
    down_result = down_step(down_result, 2, [near, *far_near])
    last, d_near, d_beside, down_result = tie(last, d_near, d_beside, down_result)
    d_near_beside = trade(d_near, 1)
    down_result = down_step(down_result, 1, [beside, *far_beside])
    down_result = down_step(down_result, 3, [near_beside, *last])
    d_far, d_near_beside, down_result = tie(d_far, d_near_beside, down_result)
    d_far_near = [trade(value, 2) for value in d_far]
    d_far_beside = [trade(value, 1) for value in d_far]
    up_result = up_step((), 0, [dpre, *d_far])
    d_far_beside, up_result = tie(d_far_beside, up_result)
    d_last = [trade(value, 2) for value in d_far_beside]
    up_result = up_step(up_result, 2, [d_near, *d_far_near])
    up_result = up_step(up_result, 1, [d_beside, *d_far_beside])
    up_result = up_step(up_result, 3, [d_near_beside, *d_last])
    return (up_result[0], down_result[0], up_result[1], down_result[1])


def solution(mesh):
    return jax.shard_map(
        on_device,
        mesh=mesh,
        in_specs=(
            P("path", None),
            P("path", None),
            P("path", None),
            P("path", None),
            P(),
            P(None, "path", "shard"),
            P(None, "path", "shard"),
            P(None, "path", "shard"),
            P(None, "path", "shard"),
        ),
        out_specs=(
            P(None, "path", "shard"),
            P(None, "path", "shard"),
            P(None, "path", "shard"),
            P(None, "path", "shard"),
        ),
        check_vma=False,
    )
```

```python
import functools

import jax
import jax.numpy as jnp
from jax import lax
from jax.experimental import pallas as pl
from jax.experimental.pallas import tpu as pltpu
from jax.sharding import PartitionSpec as P

norm_epsilon = 1e-06
hidden_epsilon = 1e-05
adam_epsilon = 0.001
inner_rate = 0.05
decay_rate = 0.1
outer_rate = 0.7
momentum_coef = 0.9
vmem_limit = 56 * 1024 * 1024
small_cost = pl.CostEstimate(flops=1, bytes_accessed=1, transcendentals=0)
gelu_coef = 0.7978845608
cubic_coef = 0.044715


def gelu_pair(values):
    inner = gelu_coef * (values + cubic_coef * values * values * values)
    tangent = jnp.tanh(inner)
    activated = 0.5 * values * (1.0 + tangent)
    slopes = 0.5 * (1.0 + tangent) + 0.5 * values * (1.0 - tangent * tangent) * gelu_coef * (
        1.0 + 3.0 * cubic_coef * values * values
    )
    return (activated, slopes)


def placing_matrix(lengths, targets, row_count, path_count, capacity, first_slot, slot_count):
    ends = jnp.cumsum(lengths)
    row_ids = jnp.arange(row_count, dtype=jnp.int32)
    doc_of_row = jnp.sum((row_ids[:, None] >= ends[None, :]).astype(jnp.int32), axis=1)
    doc_hit = doc_of_row[:, None] == jnp.arange(lengths.shape[0], dtype=jnp.int32)[None, :]
    row_path = jnp.sum(jnp.where(doc_hit, targets[None, :], 0), axis=1)
    path_hit = (row_path[:, None] == jnp.arange(path_count, dtype=jnp.int32)[None, :]).astype(
        jnp.int32
    )
    ranks = jnp.sum((jnp.cumsum(path_hit, axis=0) - 1) * path_hit, axis=1)
    slots = jnp.where(ranks < capacity, row_path * capacity + ranks, -1)
    wanted = first_slot + jnp.arange(slot_count, dtype=jnp.int32)
    return (wanted[:, None] == slots[None, :]).astype(jnp.bfloat16)


def outgoing_kernel(table_ref, *refs):
    half = len(refs) // 2
    for master_ref, out_ref in zip(refs[:half], refs[half:]):
        out_ref[...] = master_ref[...].astype(jnp.bfloat16)


def outgoing_weights(member, team, master):
    count, owned, width = master.shape
    block = width // team
    masks = range(1, team)
    return pl.pallas_call(
        outgoing_kernel,
        out_shape=[jax.ShapeDtypeStruct((count, owned, block), jnp.bfloat16) for _ in masks],
        grid_spec=pltpu.PrefetchScalarGridSpec(
            num_scalar_prefetch=1,
            grid=(count,),
            in_specs=[
                pl.BlockSpec((1, owned, block), lambda i, t, mask=mask: (i, 0, t[0] ^ mask))
                for mask in masks
            ],
            out_specs=[pl.BlockSpec((1, owned, block), lambda i, t: (i, 0, 0)) for _ in masks],
        ),
        compiler_params=pltpu.CompilerParams(vmem_limit_bytes=vmem_limit),
        cost_estimate=small_cost,
        name="outgoing_weights",
    )(member.reshape(1), *[master for _ in masks])


def arranged_kernel(team, table_ref, *refs):
    pieces, (out_ref, by_source_ref, rows_ref) = refs[: 2 * team], refs[2 * team :]
    member, group, quarter = table_ref[0], table_ref[1], table_ref[2]
    _, groups, _, _, capacity, _ = pieces[0].shape
    sources = groups * team
    owned = out_ref.shape[3]

    def collect(half):
        for mask in range(team):
            for offset in range(groups):
                source = lax.rem(group + groups - offset, groups) * team + (member ^ mask)
                by_source_ref[source] = half[mask][0, offset, 0, 0].astype(jnp.float32)

    mine = ((pl.program_id(0) // (pl.num_programs(0) // 4)) ^ quarter) % 2 == 0

    @pl.when(mine)
    def _():
        collect(pieces[:team])

    @pl.when(jnp.logical_not(mine))
    def _():
        collect(pieces[team:])

    for source in range(sources):
        rows_ref[source * capacity : (source + 1) * capacity, :] = by_source_ref[source]
    for block in range(team):
        out_ref[0, block] = rows_ref[:, block * owned : (block + 1) * owned].astype(jnp.bfloat16)


def arranged(which, table, team, paths, mine, theirs):
    _, groups, _, kept, capacity, depth = mine[0].shape
    slots = paths * capacity
    owned = depth // team
    piece = pl.BlockSpec(
        (1, groups, 1, 1, capacity, depth),
        lambda p, t: ((lax.div(p, kept) ^ t[2]) // 2, 0, which, lax.rem(p, kept), 0, 0),
    )
    return pl.pallas_call(
        functools.partial(arranged_kernel, team),
        out_shape=jax.ShapeDtypeStruct((paths, team, slots, owned), jnp.bfloat16),
        grid_spec=pltpu.PrefetchScalarGridSpec(
            num_scalar_prefetch=1,
            grid=(paths,),
            in_specs=[piece] * (2 * team),
            out_specs=pl.BlockSpec((1, team, slots, owned), lambda p, t: (p, 0, 0, 0)),
            scratch_shapes=[
                pltpu.VMEM((groups * team, capacity, depth), jnp.float32),
                pltpu.VMEM((slots, depth), jnp.float32),
            ],
        ),
        compiler_params=pltpu.CompilerParams(vmem_limit_bytes=vmem_limit),
        cost_estimate=small_cost,
        name="arranged",
    )(table, *mine, *theirs)


def product_kernel(team, listed, table_ref, rows_ref, own_ref, *refs):
    received, out_ref = refs[:-1], refs[-1]
    member = table_ref[0]
    module = table_ref[1 + listed + pl.program_id(0)]
    total = jnp.dot(
        rows_ref[0, member],
        own_ref[module].astype(jnp.bfloat16),
        preferred_element_type=jnp.float32,
    )
    for mask in range(1, team):
        total += jnp.dot(
            rows_ref[0, member ^ mask],
            received[mask - 1][module],
            preferred_element_type=jnp.float32,
        )
    out_ref[0] = total


def products(member, paths, modules, rows, master, received):
    _, team, slots, owned = rows.shape
    count, _, block = received[0].shape
    listed = paths.shape[0]
    table = jnp.concatenate([member.reshape(1), paths, jnp.take(modules, paths)])
    weights = pl.BlockSpec((count, owned, block), lambda i, t: (0, 0, 0))
    return pl.pallas_call(
        functools.partial(product_kernel, team, listed),
        out_shape=jax.ShapeDtypeStruct((listed, slots, block), jnp.float32),
        grid_spec=pltpu.PrefetchScalarGridSpec(
            num_scalar_prefetch=1,
            grid=(listed,),
            in_specs=[
                pl.BlockSpec((1, team, slots, owned), lambda i, t: (t[1 + i], 0, 0, 0)),
                pl.BlockSpec((count, owned, block), lambda i, t: (0, 0, t[0])),
            ]
            + [weights] * (team - 1),
            out_specs=pl.BlockSpec((1, slots, block), lambda i, t: (i, 0, 0)),
        ),
        compiler_params=pltpu.CompilerParams(vmem_limit_bytes=vmem_limit),
        cost_estimate=small_cost,
        name="products",
    )(table, rows, master, *received)


def update_kernel(blocks, groups, tiles, previous_count, table_ref, left_ref, *refs):
    rights = refs[: blocks * groups]
    master_ref, moment_ref = refs[blocks * groups : blocks * groups + 2]
    new_master_ref, new_moment_ref, sums_ref, decay_ref = refs[blocks * groups + 2 + previous_count :]
    paths = left_ref.shape[0]
    sums_ref[...] = jnp.zeros_like(sums_ref)
    decay_ref[...] = decay_rate * master_ref[...].astype(jnp.bfloat16).astype(jnp.float32)

    def accumulate(block):
        for group in range(groups):
            right_ref = rights[block * groups + group]
            for member in range(right_ref.shape[0]):
                path = table_ref[blocks + group] + member
                module = table_ref[blocks + groups + path]
                gradient = jnp.dot(
                    left_ref[path], right_ref[member], preferred_element_type=jnp.float32
                )
                step = gradient * pl.reciprocal(jnp.abs(gradient) + adam_epsilon)
                update = step + decay_ref[module]
                sums_ref[module] += (-inner_rate * update).astype(jnp.bfloat16).astype(jnp.float32)

    for block in range(blocks):
        pl.when(pl.program_id(0) // tiles == block)(functools.partial(accumulate, block))

    for module in range(master_ref.shape[0]):
        count = lax.fori_loop(
            0,
            paths,
            lambda path, total: total
            + (table_ref[blocks + groups + path] == module).astype(jnp.int32),
            0,
        )
        divisor = jnp.maximum(count, 1).astype(jnp.float32)
        pseudo = -sums_ref[module] / divisor
        buffer = momentum_coef * moment_ref[module].astype(jnp.float32) + pseudo
        new_master_ref[module] = master_ref[module] - outer_rate * (pseudo + momentum_coef * buffer)
        new_moment_ref[module] = buffer.astype(jnp.bfloat16)


def updated(columns, firsts, modules, left, rights, master, moment, previous):
    paths, owned, slots = left.shape
    count, _, width = master.shape
    blocks, groups = len(rights), len(rights[0])
    members, _, block = rights[0][0].shape
    tile = min(256, block)
    tiles = block // tile
    table = jnp.concatenate([jnp.stack(columns), firsts, modules])
    module_spec = pl.BlockSpec(
        (count, owned, tile),
        lambda f, t: (0, 0, t[lax.div(f, tiles)] * tiles + lax.rem(f, tiles)),
    )
    right_specs = [
        pl.BlockSpec(
            (members, slots, tile),
            lambda f, t, start=index * tiles: (0, 0, jnp.clip(f - start, 0, tiles - 1)),
        )
        for index in range(blocks)
        for _ in range(groups)
    ]
    first_previous = 4 + blocks * groups
    return pl.pallas_call(
        functools.partial(update_kernel, blocks, groups, tiles, len(previous)),
        out_shape=(
            jax.ShapeDtypeStruct(master.shape, jnp.float32),
            jax.ShapeDtypeStruct(master.shape, jnp.bfloat16),
        ),
        grid_spec=pltpu.PrefetchScalarGridSpec(
            num_scalar_prefetch=1,
            grid=(blocks * tiles,),
            in_specs=[pl.BlockSpec((paths, owned, slots), lambda f, t: (0, 0, 0))]
            + right_specs
            + [module_spec, module_spec]
            + [pl.BlockSpec(memory_space=pl.ANY)] * len(previous),
            out_specs=[module_spec, module_spec],
            scratch_shapes=[pltpu.VMEM((count, owned, tile), jnp.float32)] * 2,
        ),
        input_output_aliases={first_previous + i: i for i in range(len(previous))},
        compiler_params=pltpu.CompilerParams(vmem_limit_bytes=vmem_limit),
        cost_estimate=small_cost,
        name="updated",
    )(table, left, *[right for listed in rights for right in listed], master, moment, *previous)


def on_device(
    tokens,
    out_grad,
    doc_lengths,
    doc_paths,
    membership,
    up_master,
    down_master,
    up_moment,
    down_moment,
):
    path_count = lax.axis_size("path")
    shard_count = lax.axis_size("shard")
    row_count, features = tokens.shape
    width = up_master.shape[2]
    hidden_units = width * shard_count
    capacity = row_count // path_count
    slots = path_count * capacity
    kept = path_count // 4
    up_modules, down_modules = membership[:, 0], membership[:, 1]

    team = 4
    groups = path_count // team
    me = lax.axis_index("path")
    member, group = me % team, me // team
    quarter = lax.axis_index("shard") % 4
    bits = (2, 1)

    def trade(value, mask):
        return lax.ppermute(value, "path", [(i, i ^ mask) for i in range(path_count)])

    def move(value, offset):
        if offset == 0:
            return value
        return lax.ppermute(
            value, "path", [(i, (i + team * offset) % path_count) for i in range(path_count)]
        )

    def share(value, mask):
        return lax.ppermute(value, "shard", [(i, i ^ mask) for i in range(shard_count)])

    def tie(*values):
        return lax.optimization_barrier(values)

    up_out = outgoing_weights(member, team, up_master)
    up_beside, up_near = trade(up_out[0], 1), trade(up_out[1], 2)

    placing = placing_matrix(
        doc_lengths[0],
        doc_paths[0],
        row_count,
        path_count,
        capacity,
        quarter * kept * capacity,
        kept * capacity,
    )
    rows = jnp.dot(placing, tokens, preferred_element_type=jnp.float32)
    grads = jnp.dot(placing, out_grad, preferred_element_type=jnp.float32).astype(jnp.bfloat16)
    normed = (
        rows * lax.rsqrt(jnp.mean(rows * rows, axis=1, keepdims=True) + norm_epsilon)
    ).astype(jnp.bfloat16)
    depth = features // groups

    sent = jnp.stack([normed, grads]).reshape(2, kept, capacity, features)
    pieces = jnp.stack(
        [
            move(
                lax.dynamic_slice_in_dim(sent, (group + offset) % groups * depth, depth, 3), offset
            )
            for offset in range(groups)
        ]
    )
    near, beside, along = trade(pieces, 2), trade(pieces, 1), share(pieces, 2)
    near, beside, along, up_beside, up_near, across = tie(
        near, beside, along, up_beside, up_near, up_out[2]
    )
    up_across = trade(across, 3)
    near_beside = trade(near, 1)
    near_along, beside_along = share(near, 2), share(beside, 2)
    down_out = outgoing_weights(member, team, down_master)
    near_beside, near_along, beside_along, down_out = tie(
        near_beside, near_along, beside_along, down_out
    )
    down_near = trade(down_out[1], 2)
    mine = [
        jnp.stack(pair)
        for pair in (
            (pieces, along),
            (beside, beside_along),
            (near, near_along),
            (near_beside, share(near_beside, 2)),
        )
    ]
    theirs = [share(value, 1) for value in mine]
    down_beside, down_across = trade(down_out[0], 1), trade(down_out[2], 3)
    place = jnp.stack([member, group, quarter])

    def group_paths(offset):
        return (group + offset) % groups * team + jnp.arange(team, dtype=jnp.int32)

    def part_of(offset, rows, modules, master, weights):
        return products(member, group_paths(offset), modules, rows, master, weights)

    def summed(own, moved):
        for value in moved:
            own = own + value
        return own

    others = range(1, groups)

    def row_sums(values):
        summed = lax.psum(jnp.sum(values, axis=2), "shard")
        for bit in bits:
            summed = summed + trade(summed, bit)
        return summed

    def own_blocks(block):
        return [move(block, offset) for offset in range(groups)]

    firsts = jnp.stack([(group + groups - offset) % groups * team for offset in range(groups)])
    def outer_step(found, results, some_batches, modules, left, master, moment):
        for batch in some_batches:
            results = updated(
                [member ^ mask for mask in batch],
                firsts,
                modules,
                left,
                [found[mask] for mask in batch],
                master,
                moment,
                results,
            )
        return results

    def left_of(rows):
        return lax.dynamic_index_in_dim(rows, member, 1, False).transpose(0, 2, 1)

    def moved(block):
        return [move(block, offset) for offset in others]

    normed_rows = arranged(0, place, team, path_count, mine, theirs)
    up_operands = (normed_rows, up_modules, up_master, [up_beside, up_near, up_across])
    pre_parts = [part_of(offset, *up_operands) for offset in others]
    pre_parts, down_near = tie(pre_parts, down_near)
    pre_moved = [move(part, offset) for part, offset in zip(pre_parts, others)]
    pre_own = part_of(0, *up_operands)
    late_place, pre_own = tie(place, pre_own)
    grad_rows = arranged(1, late_place, team, path_count, mine, theirs)
    down_operands = (grad_rows, down_modules, down_master, [down_beside, down_near, down_across])
    back_parts = [part_of(offset, *down_operands) for offset in others]
    back_own = part_of(0, *down_operands)
    pre_moved, back_parts = tie(pre_moved, back_parts)
    early = 2
    back_early = [move(part[:early], offset) for part, offset in zip(back_parts, others)]

    activated, slopes = gelu_pair(summed(pre_own, pre_moved))
    scale = jnp.sqrt(row_sums(activated * activated) / hidden_units + hidden_epsilon)[:, :, None]
    hidden = activated / scale
    hidden, back_early = tie(hidden, back_early)
    hidden_b = hidden.astype(jnp.bfloat16)
    near, beside, far = trade(hidden_b, 2), trade(hidden_b, 1), moved(hidden_b)
    far, near, beside, back_parts, back_own = tie(far, near, beside, back_parts, back_own)
    back_late = [move(part[early:], offset) for part, offset in zip(back_parts, others)]
    far_near = [trade(value, 2) for value in far]
    far_beside = [trade(value, 1) for value in far]
    near_beside = trade(near, 1)

    def down_step(results, mask, right):
        return outer_step(
            {mask: right}, results, [[mask]], down_modules, lefts[1], down_master, down_moment
        )

    def up_step(results, mask, right):
        return outer_step(
            {mask: right}, results, [[mask]], up_modules, lefts[0], up_master, up_moment
        )

    lefts = left_of(normed_rows), left_of(grad_rows)
    down_result = down_step((), 0, [hidden_b, *far])
    far_near, far_beside, near_beside, lefts, down_result = tie(
        far_near, far_beside, near_beside, lefts, down_result
    )
    last = [trade(value, 1) for value in far_near]
    back_late, down_result = tie(back_late, down_result)

    back_moved = [jnp.concatenate(pair, axis=0) for pair in zip(back_early, back_late)]
    back = summed(back_own, back_moved)
    mixing = (row_sums(back * hidden) / hidden_units)[:, :, None]
    dpre = ((back - hidden * mixing) / scale * slopes).astype(jnp.bfloat16)
    d_far, d_near, d_beside = moved(dpre), trade(dpre, 2), trade(dpre, 1)
    down_result = down_step(down_result, 2, [near, *far_near])
    last, d_near, d_beside, down_result = tie(last, d_near, d_beside, down_result)
    d_near_beside = trade(d_near, 1)
    down_result = down_step(down_result, 1, [beside, *far_beside])
    down_result = down_step(down_result, 3, [near_beside, *last])
    d_far, d_near_beside, down_result = tie(d_far, d_near_beside, down_result)
    d_far_near = [trade(value, 2) for value in d_far]
    d_far_beside = [trade(value, 1) for value in d_far]
    up_result = up_step((), 0, [dpre, *d_far])
    d_far_beside, up_result = tie(d_far_beside, up_result)
    d_last = [trade(value, 2) for value in d_far_beside]
    up_result = up_step(up_result, 2, [d_near, *d_far_near])
    up_result = up_step(up_result, 1, [d_beside, *d_far_beside])
    up_result = up_step(up_result, 3, [d_near_beside, *d_last])
    return (up_result[0], down_result[0], up_result[1], down_result[1])


def solution(mesh):
    return jax.shard_map(
        on_device,
        mesh=mesh,
        in_specs=(
            P("path", None),
            P("path", None),
            P("path", None),
            P("path", None),
            P(),
            P(None, "path", "shard"),
            P(None, "path", "shard"),
            P(None, "path", "shard"),
            P(None, "path", "shard"),
        ),
        out_specs=(
            P(None, "path", "shard"),
            P(None, "path", "shard"),
            P(None, "path", "shard"),
            P(None, "path", "shard"),
        ),
        check_vma=False,
    )
```
